32 devices in a mesh: maps: 2 (over y), patch: 8 (over z, x), chan: 2 (over core).
Axes of the slice: x: 2, y: 2, z: 4, core: 2. Of those that a mesh axis runs over, the one named last changes fastest.
Arguments:
- features: bfloat16 [128, 2, 6144], P('chan', 'maps', 'patch'), parts along dimension 1, may hold values from -6 to 6
- out_grad: bfloat16 [128, 2, 6144], P('chan', 'maps', 'patch'), parts along dimension 1, may hold values from -6 to 6
- cheb_weights: bfloat16 [5, 128, 128], P(None, 'chan'), may hold values from -0.5 to 0.5
- band_offsets: int32 [6144, 8], P('patch'), may hold values from -128 to 128, as said below
- edge_weight: bfloat16 [6144, 8], P('patch'), may hold values from 0.099609375 to 10
Outputs:
- input_grad: bfloat16 [128, 2, 6144], P('chan', 'maps', 'patch'), parts along dimension 1
- weight_grad: bfloat16 [10, 128, 128], P('maps', 'chan'), parts along dimension 0
The draws below stay inside these ranges and needn't reach their ends.
There are 2 independent parts, one for each index of `maps`. The reference program is written for one: setup_inputs(seed, part) draws one part's arguments, and reference() takes and returns one part's arrays. A program takes and returns all parts, laid end to end along the dimension named above; an argument that names none is the same for every part. Nothing has to cross between parts.
Inputs may be any that keep to these rules, and one draw needn't show every extreme that they name: p + band_offsets[p, s] is a pixel of the map; some offset equals 128 and some equals -128.
All inputs are finite; a program needn't handle non-finite values.
Results may differ from the reference program's by a relative error of at most 0.006.
Values may be sent and summed in bfloat16 or wider, within the bound.
A program may use at most 64 MiB of HBM per device.

```python
import math
import jax
import jax.numpy as jnp
from jax import lax

C = 128
ORDERS = 5
SLOTS = 8
BATCH = 1
HALO = 128
NPIX = 6144


def draw_band_offsets(key, part):
    key = jax.random.fold_in(key, 11)
    key_a, key_b, key_c = jax.random.split(key, 3)
    near = jax.random.randint(key_a, (NPIX, 4), 1, 3)
    signs = jax.random.randint(key_b, (NPIX, 4), 0, 2) * 2 - 1
    far = jax.random.randint(key_c, (NPIX, 4), -HALO, HALO + 1)
    offsets = jnp.concatenate([near * signs, far], axis=1).astype(jnp.int32)
    place = jnp.arange(NPIX, dtype=jnp.int32)[:, None]
    target = jnp.clip(place + offsets, 0, NPIX - 1)
    offsets = (target - place).astype(jnp.int32)
    offsets = offsets.at[0, 7].set(HALO)
    offsets = offsets.at[NPIX - 1, 6].set(-HALO)
    return offsets


def steps_of(key, shape, shards, low, top_value):
    gain, own = 1.0, jax.random.fold_in(key, 6)
    for dim, shards_of in shards:
        steps = jnp.exp(jax.random.uniform(jax.random.fold_in(own, dim), (shards_of,), jnp.float32, low / len(shards), top_value / len(shards)))
        gain = gain * jnp.repeat(steps, shape[dim] // shards_of).reshape([-1 if axis == dim else 1 for axis in range(len(shape))])
    return gain


def gaussian(key, shape, scale, bound, cuts=(), kind=jnp.bfloat16):
    drawn = jax.random.normal(key, shape, jnp.float32) * scale
    if len(cuts) > 0:
        drawn = steps_of(key, shape, cuts, -0.22, 0.18) * drawn
    return jnp.clip(drawn, min=-bound, max=bound).astype(kind)


def setup_inputs(seed: int = 0, part: int = 0) -> dict:
    streams_of = jax.random.split(jax.random.key(seed), 6)
    part_splits = jax.random.split(jax.random.fold_in(streams_of[5], part), 6)
    features = gaussian(part_splits[0], (C, BATCH, NPIX), 1.0, 6.0, ((0, 2), (2, 8)))
    out_grad = gaussian(part_splits[1], (C, BATCH, NPIX), 1.0, 6.0, ((0, 2), (2, 8)))
    cheb_weights = gaussian(streams_of[2], (ORDERS, C, C), C ** -0.5, 0.5, ((1, 2),))
    band_offsets = draw_band_offsets(jax.random.fold_in(streams_of[5], 71), part)
    edge_weight = jnp.clip(jnp.exp(math.log(10.0) - 4.609084 * jax.random.uniform(streams_of[4], (NPIX, SLOTS), jnp.float32) ** steps_of(streams_of[4], (NPIX, SLOTS), ((0, 8),), -0.2, 0.2)), 0.099609375, 10.0).astype(jnp.bfloat16)
    return {"features": features, "out_grad": out_grad, "cheb_weights": cheb_weights, "band_offsets": band_offsets, "edge_weight": edge_weight}


def forward_op(field, offsets, norm_w):
    count = field.shape[2]
    place = jnp.arange(count, dtype=jnp.int32)
    total = jnp.zeros(field.shape, jnp.float32)
    for slot in range(SLOTS):
        picked = jnp.take(field, place + offsets[:, slot], axis=2).astype(jnp.float32)
        total = total - norm_w[:, slot] * picked
    return total


def adjoint_op(field, offsets, norm_w):
    count = field.shape[2]
    place = jnp.arange(count, dtype=jnp.int32)
    total = jnp.zeros(field.shape, jnp.float32)
    values = field.astype(jnp.float32)
    for slot in range(SLOTS):
        total = total.at[:, :, place + offsets[:, slot]].add(-norm_w[:, slot] * values)
    return total


def reference(features, out_grad, cheb_weights, band_offsets, edge_weight):
    weights_f = edge_weight.astype(jnp.float32)
    norm_w = weights_f / jnp.sum(weights_f, axis=1, keepdims=True)
    scale = 1.0 / (BATCH * NPIX) ** 0.5
    terms = [features]
    terms.append(forward_op(features, band_offsets, norm_w).astype(jnp.bfloat16))
    for order in range(2, ORDERS):
        nxt = 2.0 * forward_op(terms[order - 1], band_offsets, norm_w) - terms[order - 2].astype(jnp.float32)
        terms.append(nxt.astype(jnp.bfloat16))
    wgrads = []
    grads = []
    for order in range(ORDERS):
        part = lax.dot_general(terms[order], out_grad, (((1, 2), (1, 2)), ((), ())), preferred_element_type=jnp.float32)
        wgrads.append((part * scale).astype(jnp.bfloat16))
        back = lax.dot_general(cheb_weights[order], out_grad, (((1,), (0,)), ((), ())), preferred_element_type=jnp.float32)
        grads.append(back.astype(jnp.bfloat16))
    back_4 = grads[4]
    back_3 = (grads[3].astype(jnp.float32) + 2.0 * adjoint_op(back_4, band_offsets, norm_w)).astype(jnp.bfloat16)
    back_2 = (grads[2].astype(jnp.float32) + 2.0 * adjoint_op(back_3, band_offsets, norm_w) - back_4.astype(jnp.float32)).astype(jnp.bfloat16)
    back_1 = (grads[1].astype(jnp.float32) + 2.0 * adjoint_op(back_2, band_offsets, norm_w) - back_3.astype(jnp.float32)).astype(jnp.bfloat16)
    input_grad = (grads[0].astype(jnp.float32) + adjoint_op(back_1, band_offsets, norm_w) - back_2.astype(jnp.float32)).astype(jnp.bfloat16)
    return input_grad, jnp.stack(wgrads)
```

```python
import functools

import jax
import jax.numpy as jnp
from jax import lax
from jax.experimental import pallas as pl
from jax.experimental.pallas import tpu as pltpu
from jax.sharding import PartitionSpec as P

ORDERS = 5
SLOTS = 8
HALO = 128
FAR = (ORDERS - 1) * HALO
PAIRS = (ORDERS + 1) // 2
SPLIT = 1
MESH = pl.DeviceIdType.MESH
F32 = jnp.float32
BF16 = jnp.bfloat16


def merged(pack):
    offs = pack[0:SLOTS, :].astype(F32)
    w = pack[SLOTS : 2 * SLOTS, :].astype(F32)
    w = w / jnp.sum(w, axis=0, keepdims=True)
    total = w
    for turn in range(1, SLOTS):
        total = total + jnp.where(jnp.roll(offs, turn, axis=0) == offs, jnp.roll(w, turn, axis=0), 0.0)
    return offs, -total


def kernel(patches, fused, x_ref, g_ref, w_ref, off_ref, ew_ref, *refs):
    if fused:
        out_ref, wg_ref = refs[:2]
    else:
        out_ref, raw_ref = refs[:2]
    (pack, gext, bt, gk, fk, xp, wp, part, pin, halo_send, halo_recv, pair_send, pair_recv) = refs[2:15]
    if fused:
        rs_send, rs_recv, ag_send, ag_recv, rss, rsr, ags, agr = refs[15:]
    count = x_ref.shape[1]
    half = x_ref.shape[0]
    tiles = count // HALO
    edge = FAR // HALO
    blocks = (tiles + 2 * edge - 2) // 2
    maps = lax.axis_index("maps")
    me = lax.axis_index("patch")
    chan = lax.axis_index("chan")
    partner = (maps, me, 1 - chan)
    barrier = pltpu.get_barrier_semaphore()
    has_prev = me > 0
    has_next = me < patches - 1

    def greet(dst):
        pl.semaphore_signal(barrier, inc=1, device_id=dst, device_id_type=MESH)

    if fused:
        for d in range(1, patches):
            to = lax.rem(me + d, patches)
            greet((maps, to, chan))
            greet((maps, to, 1 - chan))
        greet(partner)
    else:
        greet((maps, lax.rem(me + 1, patches), chan))
        greet((maps, lax.rem(me + patches - 1, patches), chan))
        greet(partner)

    own = slice(FAR, FAR + count)
    left, right = slice(0, FAR), slice(FAR + count, FAR + count + FAR)
    packed = jnp.concatenate([off_ref[...].astype(F32), ew_ref[...].astype(F32)], axis=0)
    pack[:, own] = packed.astype(BF16)
    gext[:, own] = g_ref[...]

    def empty(side):
        gext[:, side] = jnp.zeros((half, FAR), BF16)
        pack[:, side] = jnp.ones((2 * SLOTS, FAR), BF16)

    pl.when(jnp.logical_not(has_prev))(functools.partial(empty, left))
    pl.when(jnp.logical_not(has_next))(functools.partial(empty, right))

    pl.semaphore_wait(barrier, 2 * patches - 1 if fused else 3)

    def copy(src, dst, send, recv, dev):
        return pltpu.make_async_remote_copy(
            src_ref=src, dst_ref=dst, send_sem=send, recv_sem=recv, device_id=dev, device_id_type=MESH
        )

    head, tail = pl.ds(FAR, FAR), pl.ds(count, FAR)
    lo, hi = pl.ds(0, FAR), pl.ds(FAR + count, FAR)
    prev_dev = (maps, lax.rem(me + patches - 1, patches), chan)
    next_dev = (maps, lax.rem(me + 1, patches), chan)
    to_prev = [
        copy(pack.at[:, head], pack.at[:, hi], halo_send.at[0], halo_recv.at[0], prev_dev),
        copy(gext.at[:, head], gext.at[:, hi], halo_send.at[1], halo_recv.at[1], prev_dev),
    ]
    to_next = [
        copy(pack.at[:, tail], pack.at[:, lo], halo_send.at[2], halo_recv.at[2], next_dev),
        copy(gext.at[:, tail], gext.at[:, lo], halo_send.at[3], halo_recv.at[3], next_dev),
    ]

    def each(copies, name):
        def run():
            for c in copies:
                getattr(c, name)()

        return run

    pl.when(has_next)(each(to_next, "start"))
    pl.when(has_prev)(each(to_prev, "start"))
    to_partner = [
        copy(x_ref, xp, pair_send.at[0], pair_recv.at[0], partner),
        copy(w_ref, wp, pair_send.at[1], pair_recv.at[1], partner),
    ]
    each(to_partner, "start")()

    step = (
        lax.broadcasted_iota(jnp.int32, (HALO, HALO), 0) - lax.broadcasted_iota(jnp.int32, (HALO, HALO), 1)
    ).astype(F32)

    def build(first, last, offs, w):
        for b in range(blocks):
            for u in range(2):
                for v in range(u, u + 3):
                    pt = 2 * b + v
                    if not first <= pt < last:
                        continue
                    cols = slice((pt - first) * HALO, (pt - first + 1) * HALO)
                    o = offs[:, cols] - float(HALO * (u + 1 - v))
                    ws = w[:, cols]
                    tile = jnp.zeros((HALO, HALO), F32)
                    for s in range(SLOTS):
                        tile = jnp.where(o[s : s + 1, :] == step, ws[s : s + 1, :], tile)
                    rows = slice(u * HALO, (u + 1) * HALO)
                    top = tile.astype(BF16)
                    bt[0, b, rows, v * HALO : (v + 1) * HALO] = top
                    if SPLIT == 2:
                        bt[1, b, rows, v * HALO : (v + 1) * HALO] = (tile - top.astype(F32)).astype(BF16)

    def turn_field(first, last):
        for t in range(first, last):
            field = gext[:, t * HALO : (t + 1) * HALO].astype(F32).T
            fk[0, t * HALO : (t + 1) * HALO, :] = field
            gk[0, t * HALO : (t + 1) * HALO, :] = field.astype(BF16)

    def apply(order, b, u0, u1):
        rows = slice(u0 * HALO, u1 * HALO)
        cols = slice(u0 * HALO, (u1 + 2) * HALO)
        base = 2 * b * HALO
        field = gk[order - 1, base + cols.start : base + cols.stop, :]
        total = jnp.dot(bt[0, b, rows, cols], field, preferred_element_type=F32)
        if SPLIT == 2:
            total = total + jnp.dot(bt[1, b, rows, cols], field, preferred_element_type=F32)
        to = slice(base + HALO + rows.start, base + HALO + rows.stop)
        if order >= 2:
            total = 2.0 * total - fk[order - 2, to, :]
        fk[order, to, :] = total
        gk[order, to, :] = total.astype(BF16)

    def sweep(order, skip=()):
        first, last = order, 2 * edge + tiles - order
        for b in range(blocks):
            u0 = 0 if 2 * b + 1 >= first else 1
            u1 = 2 if 2 * b + 3 <= last else 1
            if 2 * b + 1 + u0 >= first and 2 * b + 1 + u1 <= last and u0 < u1 and b not in skip:
                apply(order, b, u0, u1)

    for b in range(blocks):
        for part_no in range(SPLIT):
            bt[part_no, b, 0:HALO, 3 * HALO : 4 * HALO] = jnp.zeros((HALO, HALO), BF16)
            bt[part_no, b, HALO : 2 * HALO, 0:HALO] = jnp.zeros((HALO, HALO), BF16)
    build(edge, edge + tiles, *merged(pack[:, own]))
    turn_field(edge, edge + tiles)
    inner = [b for b in range(blocks) if 2 * b >= edge and 2 * b + 4 <= edge + tiles]
    for b in inner:
        apply(1, b, 0, 2)

    pl.when(has_next)(each(to_prev, "wait_recv"))
    pl.when(has_prev)(each(to_next, "wait_recv"))
    build(0, edge, *merged(pack[:, left]))
    build(edge + tiles, 2 * edge + tiles, *merged(pack[:, right]))
    turn_field(0, edge)
    turn_field(edge + tiles, 2 * edge + tiles)
    sweep(1, inner)
    for order in range(2, ORDERS):
        sweep(order)
    each(to_partner, "wait_recv")()

    grads = []
    for order in range(ORDERS):
        field = gk[order, own, :]
        grads.append(
            [
                jnp.dot(x_ref[...], field, preferred_element_type=F32),
                jnp.dot(xp[...], field, preferred_element_type=F32),
            ]
        )
    if fused:
        size = 2 * half // patches
        zero = jnp.zeros((half, half), F32)
        for side in range(2):
            for m in range(PAIRS):
                second = grads[2 * m + 1][side] if 2 * m + 1 < ORDERS else zero
                both = jnp.concatenate([grads[2 * m][side], second], axis=1).astype(BF16)
                for j in range(patches // 2):
                    rs_send[side * (patches // 2) + j, m * size : (m + 1) * size, :] = both[
                        j * size : (j + 1) * size, :
                    ]
        scatter = []
        for d in range(1, patches):
            to = lax.rem(me + d, patches)
            scatter.append(copy(rs_send.at[to], rs_recv.at[d], rss.at[d], rsr.at[d], (maps, to, chan)))
            scatter[-1].start()
    else:
        for order in range(ORDERS):
            for side in range(2):
                raw_ref[side, order] = grads[order][side]

    mine = jnp.zeros((half, count), F32)
    theirs = jnp.zeros((half, count), F32)
    nt = (((1,), (1,)), ((), ()))
    for order in range(ORDERS):
        field = gk[order, own, :]
        wm = jnp.where(chan == 0, w_ref[order, :, 0:half], w_ref[order, :, half:])
        wt = jnp.where(chan == 0, wp[order, :, 0:half], wp[order, :, half:])
        theirs = theirs + lax.dot_general(wt, field, nt, preferred_element_type=F32)
        mine = mine + lax.dot_general(wm, field, nt, preferred_element_type=F32)
    part[...] = theirs
    swap = copy(part, pin, pair_send.at[2], pair_recv.at[2], partner)
    swap.start()

    if fused:
        total = rs_send[me].astype(F32)
        for d in range(1, patches):
            scatter[d - 1].wait_recv()
            total = total + rs_recv[d].astype(F32)
        scale = 1.0 / (count * patches) ** 0.5
        ag_send[...] = (total * scale).astype(BF16)
        low = me < patches // 2
        goal = jnp.where(low, chan, 1 - chan)
        gather = []
        for d in range(1, patches):
            to = lax.rem(me + d, patches)
            gather.append(copy(ag_send, ag_recv.at[me], ags.at[d], agr.at[me], (maps, to, goal)))
            gather[-1].start()
        across = copy(ag_send, ag_recv.at[me], ags.at[0], agr.at[me], partner)
        pl.when(jnp.logical_not(low))(across.start)

        @pl.when(low)
        def _():
            ag_recv[me] = ag_send[...]

    swap.wait_recv()
    out_ref[...] = (mine + pin[...]).astype(BF16)

    if fused:
        size = 2 * half // patches
        for j in range(patches):
            arrive = copy(ag_send, ag_recv.at[j], ags.at[0], agr.at[j], partner)
            if j < patches // 2:
                pl.when(me != j)(arrive.wait_recv)
            else:
                arrive.wait_recv()
        mid = patches // 2
        for j in range(mid):
            here, there = ag_recv[j], ag_recv[mid + j]
            for order in range(ORDERS):
                rows = slice(order // 2 * size, (order // 2 + 1) * size)
                lanes = slice(order % 2 * half, (order % 2 + 1) * half)
                a, b = here[rows, lanes], there[rows, lanes]
                wg_ref[order, j * size : (j + 1) * size, :] = jnp.where(
                    chan == 0, jnp.concatenate([a, b], axis=1), jnp.concatenate([b, a], axis=1)
                )
        for c in scatter:
            c.wait_send()
        for c in gather:
            c.wait_send()
        pl.when(jnp.logical_not(low))(across.wait_send)
    pl.when(has_next)(each(to_next, "wait_send"))
    pl.when(has_prev)(each(to_prev, "wait_send"))
    each(to_partner, "wait_send")()
    swap.wait_send()


def on_device(features, out_grad, cheb_weights, band_offsets, edge_weight):
    half, _, count = features.shape
    patches = lax.axis_size("patch")
    pixels = count * patches
    size = 2 * half // patches
    fused = patches % 2 == 0 and size % 16 == 0 and size > 0
    wide = count + 2 * FAR
    blocks = (wide // HALO - 2) // 2
    outs = [jax.ShapeDtypeStruct((half, count), BF16)]
    if fused:
        outs.append(jax.ShapeDtypeStruct((ORDERS, half, 2 * half), BF16))
    else:
        outs.append(jax.ShapeDtypeStruct((2, ORDERS, half, half), F32))
    scratch = [
        pltpu.VMEM((2 * SLOTS, wide), BF16),
        pltpu.VMEM((half, wide), BF16),
        pltpu.VMEM((SPLIT, blocks, 2 * HALO, 4 * HALO), BF16),
        pltpu.VMEM((ORDERS, wide, half), BF16),
        pltpu.VMEM((ORDERS, wide, half), F32),
        pltpu.VMEM((half, count), BF16),
        pltpu.VMEM((ORDERS, half, 2 * half), BF16),
        pltpu.VMEM((half, count), F32),
        pltpu.VMEM((half, count), F32),
        pltpu.SemaphoreType.DMA((4,)),
        pltpu.SemaphoreType.DMA((4,)),
        pltpu.SemaphoreType.DMA((3,)),
        pltpu.SemaphoreType.DMA((3,)),
    ]
    if fused:
        piece = (PAIRS * size, 2 * half)
        scratch += [
            pltpu.VMEM((patches,) + piece, BF16),
            pltpu.VMEM((patches,) + piece, BF16),
            pltpu.VMEM(piece, BF16),
            pltpu.VMEM((patches,) + piece, BF16),
            pltpu.SemaphoreType.DMA((patches,)),
            pltpu.SemaphoreType.DMA((patches,)),
            pltpu.SemaphoreType.DMA((patches,)),
            pltpu.SemaphoreType.DMA((patches,)),
        ]
    vmem = pl.BlockSpec(memory_space=pltpu.VMEM)
    grad, weight = pl.pallas_call(
        functools.partial(kernel, patches, fused),
        out_shape=outs,
        in_specs=[vmem] * 5,
        out_specs=[vmem] * 2,
        scratch_shapes=scratch,
        compiler_params=pltpu.CompilerParams(
            collective_id=0, has_side_effects=True, vmem_limit_bytes=40 * 1024 * 1024
        ),
    )(
        features.reshape(half, count),
        out_grad.reshape(half, count),
        cheb_weights,
        band_offsets.T,
        edge_weight.T,
    )
    if not fused:
        weight = lax.psum(weight, "patch") * (1.0 / pixels**0.5)
        near = weight[0]
        far = lax.ppermute(weight[1], "chan", [(0, 1), (1, 0)])
        first = lax.axis_index("chan") == 0
        weight = jnp.where(
            first, jnp.concatenate([near, far], axis=2), jnp.concatenate([far, near], axis=2)
        ).astype(BF16)
    return grad.reshape(half, 1, count), weight


def solution(mesh):
    placed = (
        P("chan", "maps", "patch"),
        P("chan", "maps", "patch"),
        P(None, "chan", None),
        P("patch", None),
        P("patch", None),
    )
    return jax.shard_map(
        on_device,
        mesh=mesh,
        in_specs=placed,
        out_specs=(P("chan", "maps", "patch"), P("maps", "chan", None)),
        check_vma=False,
    )
```

```python
import functools

import jax
import jax.numpy as jnp
from jax import lax
from jax.experimental import pallas as pl
from jax.experimental.pallas import tpu as pltpu
from jax.sharding import PartitionSpec as P

ORDERS = 5
SLOTS = 8
HALO = 128
FAR = (ORDERS - 1) * HALO
PAIRS = (ORDERS + 1) // 2
MESH = pl.DeviceIdType.MESH
F32 = jnp.float32
BF16 = jnp.bfloat16


def merged(pack):
    offs = pack[0:SLOTS, :].astype(F32)
    w = pack[SLOTS : 2 * SLOTS, :].astype(F32)
    w = w / jnp.sum(w, axis=0, keepdims=True)
    total = w
    for turn in range(1, SLOTS):
        total = total + jnp.where(jnp.roll(offs, turn, axis=0) == offs, jnp.roll(w, turn, axis=0), 0.0)
    return offs, -total


def kernel(patches, fused, x_hbm, g_hbm, w_hbm, off_hbm, ew_hbm, *refs):
    if fused:
        out_ref, wg_ref = refs[:2]
    else:
        out_ref, raw_ref = refs[:2]
    (x_ref, w_ref, off_ref, ew_ref, pack, gext, bt, gk, fk, xp, wp, part, pin) = refs[2:15]
    load, halo_send, halo_recv, pair_send, pair_recv = refs[15:20]
    if fused:
        rs_send, rs_recv, ag_send, ag_recv, rss, rsr, ags, agr, rounds = refs[20:]
    half, count = x_hbm.shape
    own = slice(FAR, FAR + count)
    loads = [
        pltpu.make_async_copy(src, dst, load.at[n])
        for n, (src, dst) in enumerate(
            [
                (off_hbm, off_ref),
                (ew_hbm, ew_ref),
                (g_hbm, gext.at[:, pl.ds(FAR, count)]),
                (x_hbm, x_ref),
                (w_hbm, w_ref),
            ]
        )
    ]
    for c in loads:
        c.start()
    tiles = count // HALO
    edge = FAR // HALO
    wide_tiles = tiles + 2 * edge
    maps = lax.axis_index("maps")
    me = lax.axis_index("patch")
    chan = lax.axis_index("chan")
    partner = (maps, me, 1 - chan)
    barrier = pltpu.get_barrier_semaphore()
    has_prev = me > 0
    has_next = me < patches - 1

    def present(d):
        return jnp.logical_and(me + d >= 0, me + d < patches)

    def greet(sem, steps):
        for d in steps:
            pl.when(present(d))(
                functools.partial(
                    pl.semaphore_signal, sem, inc=1, device_id=(maps, me + d, chan), device_id_type=MESH
                )
            )

    def greeted(sem, steps, more=0):
        pl.semaphore_wait(sem, sum(present(d).astype(jnp.int32) for d in steps) + more)

    near, far = (1, -1, 2, -2), (4, -4)
    greet(barrier, near)
    pl.semaphore_signal(barrier, inc=1, device_id=partner, device_id_type=MESH)
    left, right = slice(0, FAR), slice(FAR + count, FAR + count + FAR)
    loads[0].wait()
    loads[1].wait()
    packed = jnp.concatenate([off_ref[...].astype(F32), ew_ref[...].astype(F32)], axis=0)
    pack[:, own] = packed.astype(BF16)

    def empty(side):
        gext[:, side] = jnp.zeros((half, FAR), BF16)
        pack[:, side] = jnp.ones((2 * SLOTS, FAR), BF16)

    pl.when(jnp.logical_not(has_prev))(functools.partial(empty, left))
    pl.when(jnp.logical_not(has_next))(functools.partial(empty, right))

    greeted(barrier, near, 1)

    def copy(src, dst, send, recv, dev):
        return pltpu.make_async_remote_copy(
            src_ref=src, dst_ref=dst, send_sem=send, recv_sem=recv, device_id=dev, device_id_type=MESH
        )

    head, tail = pl.ds(FAR, FAR), pl.ds(count, FAR)
    lo, hi = pl.ds(0, FAR), pl.ds(FAR + count, FAR)
    prev_dev = (maps, me - 1, chan)
    next_dev = (maps, me + 1, chan)
    to_prev = [copy(pack.at[:, head], pack.at[:, hi], halo_send.at[0], halo_recv.at[0], prev_dev)]
    to_next = [copy(pack.at[:, tail], pack.at[:, lo], halo_send.at[1], halo_recv.at[1], next_dev)]
    for c in range(1, edge + 1):
        src = g_hbm.at[:, pl.ds((c - 1) * HALO, HALO)]
        dst = gext.at[:, pl.ds(FAR + count + (c - 1) * HALO, HALO)]
        to_prev.append(copy(src, dst, halo_send.at[2 * c], halo_recv.at[2 * c], prev_dev))
        src = g_hbm.at[:, pl.ds(count - c * HALO, HALO)]
        dst = gext.at[:, pl.ds(FAR - c * HALO, HALO)]
        to_next.append(copy(src, dst, halo_send.at[2 * c + 1], halo_recv.at[2 * c + 1], next_dev))

    def each(copies, name):
        def run():
            for c in copies:
                getattr(c, name)()

        return run

    pl.when(has_next)(each(to_next, "start"))
    pl.when(has_prev)(each(to_prev, "start"))
    if fused:
        greet(rounds.at[0], near)
    to_partner = [
        copy(x_hbm, xp, pair_send.at[0], pair_recv.at[0], partner),
        copy(w_hbm, wp, pair_send.at[1], pair_recv.at[1], partner),
    ]
    each(to_partner, "start")()

    step = (
        lax.broadcasted_iota(jnp.int32, (HALO, HALO), 0) - lax.broadcasted_iota(jnp.int32, (HALO, HALO), 1)
    ).astype(F32)

    def build(first, last, offs, w):
        for pt in range(first, last):
            cols = slice((pt - first) * HALO, (pt - first + 1) * HALO)
            ws = w[:, cols]
            for qt in range(max(pt - 1, 1), min(pt + 1, wide_tiles - 2) + 1):
                o = offs[:, cols] - float(HALO * (qt - pt))
                tile = jnp.zeros((HALO, HALO), F32)
                for s in range(SLOTS):
                    tile = jnp.where(o[s : s + 1, :] == step, ws[s : s + 1, :], tile)
                at = (pt - qt + 1) * HALO
                bt[qt, :, at : at + HALO] = tile.astype(BF16)

    def turn_field(t):
        field = gext[:, t * HALO : (t + 1) * HALO].astype(F32).T
        fk[0, t * HALO : (t + 1) * HALO, :] = field
        gk[0, t * HALO : (t + 1) * HALO, :] = field.astype(BF16)

    def apply(order, t):
        field = gk[order - 1, (t - 1) * HALO : (t + 2) * HALO, :]
        total = jnp.dot(bt[t], field, preferred_element_type=F32)
        to = slice(t * HALO, (t + 1) * HALO)
        if order >= 2:
            total = 2.0 * total - fk[order - 2, to, :]
        fk[order, to, :] = total
        gk[order, to, :] = total.astype(BF16)

    done = set()

    def advance(first, last):
        for order in range(1, ORDERS):
            for t in range(max(first + order, order), min(last - order, wide_tiles - order)):
                if (order, t) not in done:
                    done.add((order, t))
                    apply(order, t)

    grads = []

    def products(order):
        field = gk[order, own, :]
        grads.append(
            [
                jnp.dot(x_ref[...], field, preferred_element_type=F32),
                jnp.dot(xp[...], field, preferred_element_type=F32),
            ]
        )

    build(edge, edge + tiles, *merged(pack[:, own]))
    loads[2].wait()
    for t in range(edge, edge + tiles):
        turn_field(t)
    advance(edge, edge + tiles)
    if fused:
        greeted(rounds.at[0], near)
        greet(rounds.at[1], far)

    pl.when(has_next)(to_prev[0].wait_recv)
    pl.when(has_prev)(to_next[0].wait_recv)
    build(0, edge, *merged(pack[:, left]))
    build(edge + tiles, wide_tiles, *merged(pack[:, right]))
    if fused:
        greeted(rounds.at[1], far)
        pl.semaphore_signal(rounds.at[2], inc=1, device_id=partner, device_id_type=MESH)
    for c in range(1, edge + 1):
        pl.when(has_next)(to_prev[c].wait_recv)
        pl.when(has_prev)(to_next[c].wait_recv)
        turn_field(edge - c)
        turn_field(edge + tiles - 1 + c)
        advance(edge - c, edge + tiles + c)
        if c == 1:
            each(to_partner, "wait_recv")()
            loads[3].wait()
            loads[4].wait()
            products(0)
        products(c)
    if fused:
        pl.semaphore_wait(rounds.at[2], 1)

    if fused:
        size = 2 * half // patches
        zero = jnp.zeros((half, half), F32)
        for side in range(2):
            for m in range(PAIRS):
                second = grads[2 * m + 1][side] if 2 * m + 1 < ORDERS else zero
                both = jnp.concatenate([grads[2 * m][side], second], axis=1).astype(BF16)
                for j in range(patches // 2):
                    rs_send[side * (patches // 2) + j, m * size : (m + 1) * size, :] = both[
                        j * size : (j + 1) * size, :
                    ]
        scatter = []
        for d in range(1, patches):
            to = lax.rem(me + d, patches)
            scatter.append(copy(rs_send.at[to], rs_recv.at[d], rss.at[d], rsr.at[d], (maps, to, chan)))
            scatter[-1].start()
    else:
        for order in range(ORDERS):
            for side in range(2):
                raw_ref[side, order] = grads[order][side]

    mine = jnp.zeros((half, count), F32)
    theirs = jnp.zeros((half, count), F32)
    nt = (((1,), (1,)), ((), ()))
    for order in range(ORDERS):
        field = gk[order, own, :]
        wm = jnp.where(chan == 0, w_ref[order, :, 0:half], w_ref[order, :, half:])
        wt = jnp.where(chan == 0, wp[order, :, 0:half], wp[order, :, half:])
        theirs = theirs + lax.dot_general(wt, field, nt, preferred_element_type=F32)
        mine = mine + lax.dot_general(wm, field, nt, preferred_element_type=F32)
    part[...] = theirs
    swap = copy(part, pin, pair_send.at[2], pair_recv.at[2], partner)
    swap.start()

    if fused:
        total = rs_send[me].astype(F32)
        for d in range(1, patches):
            scatter[d - 1].wait_recv()
            total = total + rs_recv[d].astype(F32)
        scale = 1.0 / (count * patches) ** 0.5
        ag_send[...] = (total * scale).astype(BF16)
        low = me < patches // 2
        goal = jnp.where(low, chan, 1 - chan)
        gather = []
        for d in range(1, patches):
            to = lax.rem(me + d, patches)
            gather.append(copy(ag_send, ag_recv.at[me], ags.at[d], agr.at[me], (maps, to, goal)))
            gather[-1].start()
        across = copy(ag_send, ag_recv.at[me], ags.at[0], agr.at[me], partner)
        pl.when(jnp.logical_not(low))(across.start)

        @pl.when(low)
        def _():
            ag_recv[me] = ag_send[...]

    swap.wait_recv()
    out_ref[...] = (mine + pin[...]).astype(BF16)

    if fused:
        size = 2 * half // patches
        for j in range(patches):
            arrive = copy(ag_send, ag_recv.at[j], ags.at[0], agr.at[j], partner)
            if j < patches // 2:
                pl.when(me != j)(arrive.wait_recv)
            else:
                arrive.wait_recv()
        mid = patches // 2
        for j in range(mid):
            here, there = ag_recv[j], ag_recv[mid + j]
            for order in range(ORDERS):
                rows = slice(order // 2 * size, (order // 2 + 1) * size)
                lanes = slice(order % 2 * half, (order % 2 + 1) * half)
                a, b = here[rows, lanes], there[rows, lanes]
                wg_ref[order, j * size : (j + 1) * size, :] = jnp.where(
                    chan == 0, jnp.concatenate([a, b], axis=1), jnp.concatenate([b, a], axis=1)
                )
        for c in scatter:
            c.wait_send()
        for c in gather:
            c.wait_send()
        pl.when(jnp.logical_not(low))(across.wait_send)
    pl.when(has_next)(each(to_next, "wait_send"))
    pl.when(has_prev)(each(to_prev, "wait_send"))
    each(to_partner, "wait_send")()
    swap.wait_send()


def on_device(features, out_grad, cheb_weights, band_offsets, edge_weight):
    half, _, count = features.shape
    patches = lax.axis_size("patch")
    pixels = count * patches
    size = 2 * half // patches
    fused = patches % 2 == 0 and size % 16 == 0 and size > 0
    wide = count + 2 * FAR
    outs = [jax.ShapeDtypeStruct((half, count), BF16)]
    if fused:
        outs.append(jax.ShapeDtypeStruct((ORDERS, half, 2 * half), BF16))
    else:
        outs.append(jax.ShapeDtypeStruct((2, ORDERS, half, half), F32))
    scratch = [
        pltpu.VMEM((half, count), BF16),
        pltpu.VMEM((ORDERS, half, 2 * half), BF16),
        pltpu.VMEM((SLOTS, count), jnp.int32),
        pltpu.VMEM((SLOTS, count), BF16),
        pltpu.VMEM((2 * SLOTS, wide), BF16),
        pltpu.VMEM((half, wide), BF16),
        pltpu.VMEM((wide // HALO, HALO, 3 * HALO), BF16),
        pltpu.VMEM((ORDERS, wide, half), BF16),
        pltpu.VMEM((ORDERS, wide, half), F32),
        pltpu.VMEM((half, count), BF16),
        pltpu.VMEM((ORDERS, half, 2 * half), BF16),
        pltpu.VMEM((half, count), F32),
        pltpu.VMEM((half, count), F32),
        pltpu.SemaphoreType.DMA((5,)),
        pltpu.SemaphoreType.DMA((2 * ORDERS,)),
        pltpu.SemaphoreType.DMA((2 * ORDERS,)),
        pltpu.SemaphoreType.DMA((3,)),
        pltpu.SemaphoreType.DMA((3,)),
    ]
    if fused:
        piece = (PAIRS * size, 2 * half)
        scratch += [
            pltpu.VMEM((patches,) + piece, BF16),
            pltpu.VMEM((patches,) + piece, BF16),
            pltpu.VMEM(piece, BF16),
            pltpu.VMEM((patches,) + piece, BF16),
            pltpu.SemaphoreType.DMA((patches,)),
            pltpu.SemaphoreType.DMA((patches,)),
            pltpu.SemaphoreType.DMA((patches,)),
            pltpu.SemaphoreType.DMA((patches,)),
            pltpu.SemaphoreType.REGULAR((3,)),
        ]
    vmem = pl.BlockSpec(memory_space=pltpu.VMEM)
    grad, weight = pl.pallas_call(
        functools.partial(kernel, patches, fused),
        out_shape=outs,
        in_specs=[pl.BlockSpec(memory_space=pltpu.HBM)] * 5,
        out_specs=[vmem] * 2,
        scratch_shapes=scratch,
        compiler_params=pltpu.CompilerParams(
            collective_id=0, has_side_effects=True, vmem_limit_bytes=63 * 1024 * 1024
        ),
    )(
        features.reshape(half, count),
        out_grad.reshape(half, count),
        cheb_weights,
        band_offsets.T,
        edge_weight.T,
    )
    if not fused:
        weight = lax.psum(weight, "patch") * (1.0 / pixels**0.5)
        near = weight[0]
        far = lax.ppermute(weight[1], "chan", [(0, 1), (1, 0)])
        first = lax.axis_index("chan") == 0
        weight = jnp.where(
            first, jnp.concatenate([near, far], axis=2), jnp.concatenate([far, near], axis=2)
        ).astype(BF16)
    return grad.reshape(half, 1, count), weight


def solution(mesh):
    placed = (
        P("chan", "maps", "patch"),
        P("chan", "maps", "patch"),
        P(None, "chan", None),
        P("patch", None),
        P("patch", None),
    )
    return jax.shard_map(
        on_device,
        mesh=mesh,
        in_specs=placed,
        out_specs=(P("chan", "maps", "patch"), P("maps", "chan", None)),
        check_vma=False,
    )
```

```python
import functools

import jax
import jax.numpy as jnp
from jax import lax
from jax.experimental import pallas as pl
from jax.experimental.pallas import tpu as pltpu
from jax.sharding import PartitionSpec as P

ORDERS = 5
SLOTS = 8
HALO = 128
FAR = (ORDERS - 1) * HALO
PAIRS = (ORDERS + 1) // 2
MESH = pl.DeviceIdType.MESH
F32 = jnp.float32
BF16 = jnp.bfloat16


def merged(pack):
    offs = pack[0:SLOTS, :].astype(F32)
    w = pack[SLOTS : 2 * SLOTS, :].astype(F32)
    w = w / jnp.sum(w, axis=0, keepdims=True)
    total = w
    for turn in range(1, SLOTS):
        total = total + jnp.where(jnp.roll(offs, turn, axis=0) == offs, jnp.roll(w, turn, axis=0), 0.0)
    return offs, -total


def kernel(patches, fused, x_hbm, g_hbm, w_hbm, off_hbm, ew_hbm, *refs):
    if fused:
        out_ref, wg_ref = refs[:2]
    else:
        out_ref, raw_ref = refs[:2]
    (x_ref, w_ref, off_ref, ew_ref, pack, gext, bt, gk, fk, xp, wp, part, pin) = refs[2:15]
    load, halo_send, halo_recv, pair_send, pair_recv = refs[15:20]
    if fused:
        rs_send, rs_recv, ag_send, ag_recv, rss, rsr, ags, agr, rounds = refs[20:]
    half, count = x_hbm.shape
    own = slice(FAR, FAR + count)
    loads = [
        pltpu.make_async_copy(src, dst, load.at[n])
        for n, (src, dst) in enumerate(
            [
                (off_hbm, off_ref),
                (ew_hbm, ew_ref),
                (g_hbm, gext.at[:, pl.ds(FAR, count)]),
                (x_hbm, x_ref),
                (w_hbm, w_ref),
            ]
        )
    ]
    for c in loads:
        c.start()
    tiles = count // HALO
    edge = FAR // HALO
    wide_tiles = tiles + 2 * edge
    maps = lax.axis_index("maps")
    me = lax.axis_index("patch")
    chan = lax.axis_index("chan")
    partner = (maps, me, 1 - chan)
    barrier = pltpu.get_barrier_semaphore()
    has_prev = me > 0
    has_next = me < patches - 1

    def present(d):
        return jnp.logical_and(me + d >= 0, me + d < patches)

    def greet(sem, steps):
        for d in steps:
            pl.when(present(d))(
                functools.partial(
                    pl.semaphore_signal, sem, inc=1, device_id=(maps, me + d, chan), device_id_type=MESH
                )
            )

    def greeted(sem, steps, more=0):
        pl.semaphore_wait(sem, sum(present(d).astype(jnp.int32) for d in steps) + more)

    near, far = (1, -1, 2, -2), (4, -4)
    greet(barrier, near)
    pl.semaphore_signal(barrier, inc=1, device_id=partner, device_id_type=MESH)
    left, right = slice(0, FAR), slice(FAR + count, FAR + count + FAR)
    loads[0].wait()
    loads[1].wait()
    packed = jnp.concatenate([off_ref[...].astype(F32), ew_ref[...].astype(F32)], axis=0)
    pack[:, own] = packed.astype(BF16)

    def empty(side):
        gext[:, side] = jnp.zeros((half, FAR), BF16)
        pack[:, side] = jnp.ones((2 * SLOTS, FAR), BF16)

    pl.when(jnp.logical_not(has_prev))(functools.partial(empty, left))
    pl.when(jnp.logical_not(has_next))(functools.partial(empty, right))

    greeted(barrier, near, 1)

    def copy(src, dst, send, recv, dev):
        return pltpu.make_async_remote_copy(
            src_ref=src, dst_ref=dst, send_sem=send, recv_sem=recv, device_id=dev, device_id_type=MESH
        )

    head, tail = pl.ds(FAR, FAR), pl.ds(count, FAR)
    lo, hi = pl.ds(0, FAR), pl.ds(FAR + count, FAR)
    prev_dev = (maps, me - 1, chan)
    next_dev = (maps, me + 1, chan)
    to_prev = [copy(pack.at[:, head], pack.at[:, hi], halo_send.at[0], halo_recv.at[0], prev_dev)]
    to_next = [copy(pack.at[:, tail], pack.at[:, lo], halo_send.at[1], halo_recv.at[1], next_dev)]
    src = g_hbm.at[:, pl.ds(0, FAR)]
    to_prev.append(copy(src, gext.at[:, hi], halo_send.at[2], halo_recv.at[2], prev_dev))
    src = g_hbm.at[:, pl.ds(count - FAR, FAR)]
    to_next.append(copy(src, gext.at[:, lo], halo_send.at[3], halo_recv.at[3], next_dev))

    def each(copies, name):
        def run():
            for c in copies:
                getattr(c, name)()

        return run

    pl.when(has_next)(each(to_next, "start"))
    pl.when(has_prev)(each(to_prev, "start"))
    if fused:
        greet(rounds.at[0], near)
    to_partner = [
        copy(x_hbm, xp, pair_send.at[0], pair_recv.at[0], partner),
        copy(w_hbm, wp, pair_send.at[1], pair_recv.at[1], partner),
    ]
    each(to_partner, "start")()

    nt = (((1,), (1,)), ((), ()))
    step = (
        lax.broadcasted_iota(jnp.int32, (HALO, HALO), 0) - lax.broadcasted_iota(jnp.int32, (HALO, HALO), 1)
    ).astype(F32)

    def build(first, last, offs, w):
        for pt in range(first, last):
            cols = slice((pt - first) * HALO, (pt - first + 1) * HALO)
            ws = w[:, cols]
            for qt in range(max(pt - 1, 1), min(pt + 1, wide_tiles - 2) + 1):
                o = offs[:, cols] - float(HALO * (qt - pt))
                tile = jnp.zeros((HALO, HALO), F32)
                for s in range(SLOTS):
                    tile = jnp.where(o[s : s + 1, :] == step, ws[s : s + 1, :], tile)
                at = (pt - qt + 1) * HALO
                bt[qt, :, at : at + HALO] = tile.astype(BF16)

    def turn_field(t):
        field = gext[:, t * HALO : (t + 1) * HALO]
        fk[0, :, t * HALO : (t + 1) * HALO] = field.astype(F32)
        gk[0, :, t * HALO : (t + 1) * HALO] = field

    def apply(order, t):
        field = gk[order - 1, :, (t - 1) * HALO : (t + 2) * HALO]
        total = lax.dot_general(field, bt[t], nt, preferred_element_type=F32)
        to = slice(t * HALO, (t + 1) * HALO)
        if order >= 2:
            total = 2.0 * total - fk[order - 2, :, to]
        fk[order, :, to] = total
        gk[order, :, to] = total.astype(BF16)

    done = set()

    def advance(first, last):
        for order in range(1, ORDERS):
            for t in range(max(first + order, order), min(last - order, wide_tiles - order)):
                if (order, t) not in done:
                    done.add((order, t))
                    apply(order, t)

    grads = []

    def products(order):
        field = gk[order, :, own]
        grads.append(
            [
                lax.dot_general(x_ref[...], field, nt, preferred_element_type=F32),
                lax.dot_general(xp[...], field, nt, preferred_element_type=F32),
            ]
        )

    build(edge, edge + tiles, *merged(pack[:, own]))
    loads[2].wait()
    for t in range(edge, edge + tiles):
        turn_field(t)
    advance(edge, edge + tiles)
    if fused:
        greeted(rounds.at[0], near)
        greet(rounds.at[1], far)

    pl.when(has_next)(to_prev[0].wait_recv)
    pl.when(has_prev)(to_next[0].wait_recv)
    build(0, edge, *merged(pack[:, left]))
    build(edge + tiles, wide_tiles, *merged(pack[:, right]))
    if fused:
        greeted(rounds.at[1], far)
        pl.semaphore_signal(rounds.at[2], inc=1, device_id=partner, device_id_type=MESH)
    each(to_partner, "wait_recv")()
    loads[3].wait()
    loads[4].wait()
    products(0)
    pl.when(has_next)(to_prev[1].wait_recv)
    pl.when(has_prev)(to_next[1].wait_recv)
    for t in range(edge):
        turn_field(t)
        turn_field(edge + tiles + t)
    advance(0, wide_tiles)
    for order in range(1, ORDERS):
        products(order)
    if fused:
        pl.semaphore_wait(rounds.at[2], 1)

    if fused:
        size = 2 * half // patches
        zero = jnp.zeros((half, half), F32)
        for side in range(2):
            for m in range(PAIRS):
                second = grads[2 * m + 1][side] if 2 * m + 1 < ORDERS else zero
                both = jnp.concatenate([grads[2 * m][side], second], axis=1).astype(BF16)
                for j in range(patches // 2):
                    rs_send[side * (patches // 2) + j, m * size : (m + 1) * size, :] = both[
                        j * size : (j + 1) * size, :
                    ]
        scatter = []
        for d in range(1, patches):
            to = lax.rem(me + d, patches)
            scatter.append(copy(rs_send.at[to], rs_recv.at[d], rss.at[d], rsr.at[d], (maps, to, chan)))
            scatter[-1].start()
    else:
        for order in range(ORDERS):
            for side in range(2):
                raw_ref[side, order] = grads[order][side]

    mine = jnp.zeros((half, count), F32)
    theirs = jnp.zeros((half, count), F32)
    for order in range(ORDERS):
        field = gk[order, :, own]
        wm = jnp.where(chan == 0, w_ref[order, :, 0:half], w_ref[order, :, half:])
        wt = jnp.where(chan == 0, wp[order, :, 0:half], wp[order, :, half:])
        theirs = theirs + jnp.dot(wt, field, preferred_element_type=F32)
        mine = mine + jnp.dot(wm, field, preferred_element_type=F32)
    part[...] = theirs
    swap = copy(part, pin, pair_send.at[2], pair_recv.at[2], partner)
    swap.start()

    if fused:
        total = rs_send[me].astype(F32)
        for d in range(1, patches):
            scatter[d - 1].wait_recv()
            total = total + rs_recv[d].astype(F32)
        scale = 1.0 / (count * patches) ** 0.5
        ag_send[...] = (total * scale).astype(BF16)
        low = me < patches // 2
        goal = jnp.where(low, chan, 1 - chan)
        gather = []
        for d in range(1, patches):
            to = lax.rem(me + d, patches)
            gather.append(copy(ag_send, ag_recv.at[me], ags.at[d], agr.at[me], (maps, to, goal)))
            gather[-1].start()
        across = copy(ag_send, ag_recv.at[me], ags.at[0], agr.at[me], partner)
        pl.when(jnp.logical_not(low))(across.start)

        @pl.when(low)
        def _():
            ag_recv[me] = ag_send[...]

    swap.wait_recv()
    out_ref[...] = (mine + pin[...]).astype(BF16)

    if fused:
        size = 2 * half // patches
        for j in range(patches):
            arrive = copy(ag_send, ag_recv.at[j], ags.at[0], agr.at[j], partner)
            if j < patches // 2:
                pl.when(me != j)(arrive.wait_recv)
            else:
                arrive.wait_recv()
        mid = patches // 2
        for j in range(mid):
            here, there = ag_recv[j], ag_recv[mid + j]
            for order in range(ORDERS):
                rows = slice(order // 2 * size, (order // 2 + 1) * size)
                lanes = slice(order % 2 * half, (order % 2 + 1) * half)
                a, b = here[rows, lanes], there[rows, lanes]
                wg_ref[order, j * size : (j + 1) * size, :] = jnp.where(
                    chan == 0, jnp.concatenate([a, b], axis=1), jnp.concatenate([b, a], axis=1)
                )
        for c in scatter:
            c.wait_send()
        for c in gather:
            c.wait_send()
        pl.when(jnp.logical_not(low))(across.wait_send)
    pl.when(has_next)(each(to_next, "wait_send"))
    pl.when(has_prev)(each(to_prev, "wait_send"))
    each(to_partner, "wait_send")()
    swap.wait_send()


def on_device(features, out_grad, cheb_weights, band_offsets, edge_weight):
    half, _, count = features.shape
    patches = lax.axis_size("patch")
    pixels = count * patches
    size = 2 * half // patches
    fused = patches % 2 == 0 and size % 16 == 0 and size > 0
    wide = count + 2 * FAR
    outs = [jax.ShapeDtypeStruct((half, count), BF16)]
    if fused:
        outs.append(jax.ShapeDtypeStruct((ORDERS, half, 2 * half), BF16))
    else:
        outs.append(jax.ShapeDtypeStruct((2, ORDERS, half, half), F32))
    scratch = [
        pltpu.VMEM((half, count), BF16),
        pltpu.VMEM((ORDERS, half, 2 * half), BF16),
        pltpu.VMEM((SLOTS, count), jnp.int32),
        pltpu.VMEM((SLOTS, count), BF16),
        pltpu.VMEM((2 * SLOTS, wide), BF16),
        pltpu.VMEM((half, wide), BF16),
        pltpu.VMEM((wide // HALO, HALO, 3 * HALO), BF16),
        pltpu.VMEM((ORDERS, half, wide), BF16),
        pltpu.VMEM((ORDERS, half, wide), F32),
        pltpu.VMEM((half, count), BF16),
        pltpu.VMEM((ORDERS, half, 2 * half), BF16),
        pltpu.VMEM((half, count), F32),
        pltpu.VMEM((half, count), F32),
        pltpu.SemaphoreType.DMA((5,)),
        pltpu.SemaphoreType.DMA((4,)),
        pltpu.SemaphoreType.DMA((4,)),
        pltpu.SemaphoreType.DMA((3,)),
        pltpu.SemaphoreType.DMA((3,)),
    ]
    if fused:
        piece = (PAIRS * size, 2 * half)
        scratch += [
            pltpu.VMEM((patches,) + piece, BF16),
            pltpu.VMEM((patches,) + piece, BF16),
            pltpu.VMEM(piece, BF16),
            pltpu.VMEM((patches,) + piece, BF16),
            pltpu.SemaphoreType.DMA((patches,)),
            pltpu.SemaphoreType.DMA((patches,)),
            pltpu.SemaphoreType.DMA((patches,)),
            pltpu.SemaphoreType.DMA((patches,)),
            pltpu.SemaphoreType.REGULAR((3,)),
        ]
    vmem = pl.BlockSpec(memory_space=pltpu.VMEM)
    grad, weight = pl.pallas_call(
        functools.partial(kernel, patches, fused),
        out_shape=outs,
        in_specs=[pl.BlockSpec(memory_space=pltpu.HBM)] * 5,
        out_specs=[vmem] * 2,
        scratch_shapes=scratch,
        compiler_params=pltpu.CompilerParams(
            collective_id=0, has_side_effects=True, vmem_limit_bytes=63 * 1024 * 1024
        ),
    )(
        features.reshape(half, count),
        out_grad.reshape(half, count),
        cheb_weights,
        band_offsets.T,
        edge_weight.T,
    )
    if not fused:
        weight = lax.psum(weight, "patch") * (1.0 / pixels**0.5)
        near = weight[0]
        far = lax.ppermute(weight[1], "chan", [(0, 1), (1, 0)])
        first = lax.axis_index("chan") == 0
        weight = jnp.where(
            first, jnp.concatenate([near, far], axis=2), jnp.concatenate([far, near], axis=2)
        ).astype(BF16)
    return grad.reshape(half, 1, count), weight


def solution(mesh):
    placed = (
        P("chan", "maps", "patch"),
        P("chan", "maps", "patch"),
        P(None, "chan", None),
        P("patch", None),
        P("patch", None),
    )
    return jax.shard_map(
        on_device,
        mesh=mesh,
        in_specs=placed,
        out_specs=(P("chan", "maps", "patch"), P("maps", "chan", None)),
        check_vma=False,
    )
```

```python
import functools

import jax
import jax.numpy as jnp
from jax import lax
from jax.experimental import pallas as pl
from jax.experimental.pallas import tpu as pltpu
from jax.sharding import PartitionSpec as P

ORDERS = 5
SLOTS = 8
HALO = 128
FAR = (ORDERS - 1) * HALO
PAIRS = (ORDERS + 1) // 2
MESH = pl.DeviceIdType.MESH
F32 = jnp.float32
BF16 = jnp.bfloat16


def merged(pack):
    offs = pack[0:SLOTS, :].astype(F32)
    w = pack[SLOTS : 2 * SLOTS, :].astype(F32)
    w = w / jnp.sum(w, axis=0, keepdims=True)
    total = w
    for turn in range(1, SLOTS):
        total = total + jnp.where(jnp.roll(offs, turn, axis=0) == offs, jnp.roll(w, turn, axis=0), 0.0)
    return offs, -total


def kernel(patches, fused, x_hbm, g_hbm, w_hbm, off_hbm, ew_hbm, *refs):
    if fused:
        out_hbm, wg_hbm = refs[:2]
    else:
        out_hbm, wg_hbm = refs[:2]
    (out_ref, wg_ref, store, x_ref, w_ref, off_ref, ew_ref, pack, gext, bt, gk, fk, xp, wp, part, pin) = refs[2:18]
    load, halo_send, halo_recv, pair_send, pair_recv = refs[18:23]
    if fused:
        rs_send, rs_recv, ag_send, ag_recv, rss, rsr, ags, agr, rounds = refs[23:]
    half, count = x_hbm.shape
    own = slice(FAR, FAR + count)
    loads = [
        pltpu.make_async_copy(src, dst, load.at[n])
        for n, (src, dst) in enumerate(
            [
                (off_hbm, off_ref),
                (ew_hbm, ew_ref),
                (g_hbm, gext.at[:, pl.ds(FAR, count)]),
                (x_hbm, x_ref),
                (w_hbm, w_ref),
            ]
        )
    ]
    for c in loads:
        c.start()
    tiles = count // HALO
    edge = FAR // HALO
    wide_tiles = tiles + 2 * edge
    maps = lax.axis_index("maps")
    me = lax.axis_index("patch")
    chan = lax.axis_index("chan")
    partner = (maps, me, 1 - chan)
    barrier = pltpu.get_barrier_semaphore()
    has_prev = me > 0
    has_next = me < patches - 1

    def present(d):
        return jnp.logical_and(me + d >= 0, me + d < patches)

    def greet(sem, steps):
        for d in steps:
            pl.when(present(d))(
                functools.partial(
                    pl.semaphore_signal, sem, inc=1, device_id=(maps, me + d, chan), device_id_type=MESH
                )
            )

    def greeted(sem, steps, more=0):
        pl.semaphore_wait(sem, sum(present(d).astype(jnp.int32) for d in steps) + more)

    near, far = (1, -1, 2, -2), (4, -4)
    greet(barrier, near)
    pl.semaphore_signal(barrier, inc=1, device_id=partner, device_id_type=MESH)
    left, right = slice(0, FAR), slice(FAR + count, FAR + count + FAR)
    loads[0].wait()
    loads[1].wait()
    packed = jnp.concatenate([off_ref[...].astype(F32), ew_ref[...].astype(F32)], axis=0)
    pack[:, own] = packed.astype(BF16)

    def empty(side):
        gext[:, side] = jnp.zeros((half, FAR), BF16)
        pack[:, side] = jnp.ones((2 * SLOTS, FAR), BF16)

    pl.when(jnp.logical_not(has_prev))(functools.partial(empty, left))
    pl.when(jnp.logical_not(has_next))(functools.partial(empty, right))

    greeted(barrier, near, 1)

    def copy(src, dst, send, recv, dev):
        return pltpu.make_async_remote_copy(
            src_ref=src, dst_ref=dst, send_sem=send, recv_sem=recv, device_id=dev, device_id_type=MESH
        )

    head, tail = pl.ds(FAR, FAR), pl.ds(count, FAR)
    lo, hi = pl.ds(0, FAR), pl.ds(FAR + count, FAR)
    prev_dev = (maps, me - 1, chan)
    next_dev = (maps, me + 1, chan)
    to_prev = [copy(pack.at[:, head], pack.at[:, hi], halo_send.at[0], halo_recv.at[0], prev_dev)]
    to_next = [copy(pack.at[:, tail], pack.at[:, lo], halo_send.at[1], halo_recv.at[1], next_dev)]
    src = g_hbm.at[:, pl.ds(0, FAR)]
    to_prev.append(copy(src, gext.at[:, hi], halo_send.at[2], halo_recv.at[2], prev_dev))
    src = g_hbm.at[:, pl.ds(count - FAR, FAR)]
    to_next.append(copy(src, gext.at[:, lo], halo_send.at[3], halo_recv.at[3], next_dev))

    def each(copies, name):
        def run():
            for c in copies:
                getattr(c, name)()

        return run

    pl.when(has_next)(each(to_next, "start"))
    pl.when(has_prev)(each(to_prev, "start"))
    if fused:
        greet(rounds.at[0], near)
    to_partner = [
        copy(x_hbm, xp, pair_send.at[0], pair_recv.at[0], partner),
        copy(w_hbm, wp, pair_send.at[1], pair_recv.at[1], partner),
    ]
    each(to_partner, "start")()

    nt = (((1,), (1,)), ((), ()))
    step = (
        lax.broadcasted_iota(jnp.int32, (HALO, HALO), 0) - lax.broadcasted_iota(jnp.int32, (HALO, HALO), 1)
    ).astype(F32)

    def build(first, last, offs, w):
        for pt in range(first, last):
            cols = slice((pt - first) * HALO, (pt - first + 1) * HALO)
            ws = w[:, cols]
            for qt in range(max(pt - 1, 1), min(pt + 1, wide_tiles - 2) + 1):
                o = offs[:, cols] - float(HALO * (qt - pt))
                tile = jnp.zeros((HALO, HALO), F32)
                for s in range(SLOTS):
                    tile = jnp.where(o[s : s + 1, :] == step, ws[s : s + 1, :], tile)
                at = (pt - qt + 1) * HALO
                bt[qt, :, at : at + HALO] = tile.astype(BF16)

    def turn_field(t):
        field = gext[:, t * HALO : (t + 1) * HALO]
        fk[0, :, t * HALO : (t + 1) * HALO] = field.astype(F32)
        gk[0, :, t * HALO : (t + 1) * HALO] = field

    def apply(order, t):
        field = gk[order - 1, :, (t - 1) * HALO : (t + 2) * HALO]
        total = lax.dot_general(field, bt[t], nt, preferred_element_type=F32)
        to = slice(t * HALO, (t + 1) * HALO)
        if order >= 2:
            total = 2.0 * total - fk[order - 2, :, to]
        fk[order, :, to] = total
        gk[order, :, to] = total.astype(BF16)

    done = set()

    def advance(first, last):
        for order in range(1, ORDERS):
            for t in range(max(first + order, order), min(last - order, wide_tiles - order)):
                if (order, t) not in done:
                    done.add((order, t))
                    apply(order, t)

    grads = []

    def products(order):
        field = gk[order, :, own]
        grads.append(
            [
                lax.dot_general(x_ref[...], field, nt, preferred_element_type=F32),
                lax.dot_general(xp[...], field, nt, preferred_element_type=F32),
            ]
        )

    build(edge, edge + tiles, *merged(pack[:, own]))
    loads[2].wait()
    for t in range(edge, edge + tiles):
        turn_field(t)
    advance(edge, edge + tiles)
    if fused:
        greeted(rounds.at[0], near)
        greet(rounds.at[1], far)

    pl.when(has_next)(to_prev[0].wait_recv)
    pl.when(has_prev)(to_next[0].wait_recv)
    build(0, edge, *merged(pack[:, left]))
    build(edge + tiles, wide_tiles, *merged(pack[:, right]))
    if fused:
        greeted(rounds.at[1], far)
        pl.semaphore_signal(rounds.at[2], inc=1, device_id=partner, device_id_type=MESH)
    each(to_partner, "wait_recv")()
    loads[3].wait()
    loads[4].wait()
    products(0)
    pl.when(has_next)(to_prev[1].wait_recv)
    pl.when(has_prev)(to_next[1].wait_recv)
    for t in range(edge):
        turn_field(t)
        turn_field(edge + tiles + t)
    advance(0, wide_tiles)
    for order in range(1, ORDERS):
        products(order)
    if fused:
        pl.semaphore_wait(rounds.at[2], 1)

    if fused:
        size = 2 * half // patches
        zero = jnp.zeros((half, half), F32)
        for side in range(2):
            for m in range(PAIRS):
                second = grads[2 * m + 1][side] if 2 * m + 1 < ORDERS else zero
                both = jnp.concatenate([grads[2 * m][side], second], axis=1).astype(BF16)
                for j in range(patches // 2):
                    rs_send[side * (patches // 2) + j, m * size : (m + 1) * size, :] = both[
                        j * size : (j + 1) * size, :
                    ]
        order_of = sorted(range(1, patches), key=lambda d: -min(d, patches - d))
        scatter = []
        for d in order_of:
            to = lax.rem(me + d, patches)
            scatter.append(copy(rs_send.at[to], rs_recv.at[d], rss.at[d], rsr.at[d], (maps, to, chan)))
            scatter[-1].start()
    else:
        for order in range(ORDERS):
            for side in range(2):
                wg_ref[side, order] = grads[order][side]

    mine = jnp.zeros((half, count), F32)
    theirs = jnp.zeros((half, count), F32)
    for order in range(ORDERS):
        field = gk[order, :, own]
        wm = jnp.where(chan == 0, w_ref[order, :, 0:half], w_ref[order, :, half:])
        wt = jnp.where(chan == 0, wp[order, :, 0:half], wp[order, :, half:])
        theirs = theirs + jnp.dot(wt, field, preferred_element_type=F32)
        mine = mine + jnp.dot(wm, field, preferred_element_type=F32)
    part[...] = theirs
    swap = copy(part, pin, pair_send.at[2], pair_recv.at[2], partner)
    swap.start()

    if fused:
        total = rs_send[me].astype(F32)
        for c, d in zip(scatter, order_of):
            c.wait_recv()
            total = total + rs_recv[d].astype(F32)
        scale = 1.0 / (count * patches) ** 0.5
        ag_send[...] = (total * scale).astype(BF16)
        low = me < patches // 2
        goal = jnp.where(low, chan, 1 - chan)
        gather = []
        for d in order_of:
            to = lax.rem(me + d, patches)
            gather.append(copy(ag_send, ag_recv.at[me], ags.at[d], agr.at[me], (maps, to, goal)))
            gather[-1].start()
        across = copy(ag_send, ag_recv.at[me], ags.at[0], agr.at[me], partner)
        pl.when(jnp.logical_not(low))(across.start)

        @pl.when(low)
        def _():
            ag_recv[me] = ag_send[...]

    swap.wait_recv()
    out_ref[...] = (mine + pin[...]).astype(BF16)
    save_out = pltpu.make_async_copy(out_ref, out_hbm, store.at[0])
    save_out.start()
    save_wg = pltpu.make_async_copy(wg_ref, wg_hbm, store.at[1])

    if fused:
        size = 2 * half // patches
        for j in range(patches):
            arrive = copy(ag_send, ag_recv.at[j], ags.at[0], agr.at[j], partner)
            if j < patches // 2:
                pl.when(me != j)(arrive.wait_recv)
            else:
                arrive.wait_recv()
        mid = patches // 2
        for j in range(mid):
            here, there = ag_recv[j], ag_recv[mid + j]
            for order in range(ORDERS):
                rows = slice(order // 2 * size, (order // 2 + 1) * size)
                lanes = slice(order % 2 * half, (order % 2 + 1) * half)
                a, b = here[rows, lanes], there[rows, lanes]
                wg_ref[order, j * size : (j + 1) * size, :] = jnp.where(
                    chan == 0, jnp.concatenate([a, b], axis=1), jnp.concatenate([b, a], axis=1)
                )
        save_wg.start()
        for c in scatter:
            c.wait_send()
        for c in gather:
            c.wait_send()
        pl.when(jnp.logical_not(low))(across.wait_send)
    pl.when(has_next)(each(to_next, "wait_send"))
    pl.when(has_prev)(each(to_prev, "wait_send"))
    each(to_partner, "wait_send")()
    swap.wait_send()
    if not fused:
        save_wg.start()
    save_out.wait()
    save_wg.wait()


def on_device(features, out_grad, cheb_weights, band_offsets, edge_weight):
    half, _, count = features.shape
    patches = lax.axis_size("patch")
    pixels = count * patches
    size = 2 * half // patches
    fused = patches % 2 == 0 and size % 16 == 0 and size > 0
    wide = count + 2 * FAR
    outs = [jax.ShapeDtypeStruct((half, count), BF16)]
    if fused:
        outs.append(jax.ShapeDtypeStruct((ORDERS, half, 2 * half), BF16))
    else:
        outs.append(jax.ShapeDtypeStruct((2, ORDERS, half, half), F32))
    scratch = [
        pltpu.VMEM(outs[0].shape, outs[0].dtype),
        pltpu.VMEM(outs[1].shape, outs[1].dtype),
        pltpu.SemaphoreType.DMA((2,)),
        pltpu.VMEM((half, count), BF16),
        pltpu.VMEM((ORDERS, half, 2 * half), BF16),
        pltpu.VMEM((SLOTS, count), jnp.int32),
        pltpu.VMEM((SLOTS, count), BF16),
        pltpu.VMEM((2 * SLOTS, wide), BF16),
        pltpu.VMEM((half, wide), BF16),
        pltpu.VMEM((wide // HALO, HALO, 3 * HALO), BF16),
        pltpu.VMEM((ORDERS, half, wide), BF16),
        pltpu.VMEM((ORDERS, half, wide), F32),
        pltpu.VMEM((half, count), BF16),
        pltpu.VMEM((ORDERS, half, 2 * half), BF16),
        pltpu.VMEM((half, count), F32),
        pltpu.VMEM((half, count), F32),
        pltpu.SemaphoreType.DMA((5,)),
        pltpu.SemaphoreType.DMA((4,)),
        pltpu.SemaphoreType.DMA((4,)),
        pltpu.SemaphoreType.DMA((3,)),
        pltpu.SemaphoreType.DMA((3,)),
    ]
    if fused:
        piece = (PAIRS * size, 2 * half)
        scratch += [
            pltpu.VMEM((patches,) + piece, BF16),
            pltpu.VMEM((patches,) + piece, BF16),
            pltpu.VMEM(piece, BF16),
            pltpu.VMEM((patches,) + piece, BF16),
            pltpu.SemaphoreType.DMA((patches,)),
            pltpu.SemaphoreType.DMA((patches,)),
            pltpu.SemaphoreType.DMA((patches,)),
            pltpu.SemaphoreType.DMA((patches,)),
            pltpu.SemaphoreType.REGULAR((3,)),
        ]
    hbm = pl.BlockSpec(memory_space=pltpu.HBM)
    grad, weight = pl.pallas_call(
        functools.partial(kernel, patches, fused),
        out_shape=outs,
        in_specs=[hbm] * 5,
        out_specs=[hbm] * 2,
        scratch_shapes=scratch,
        compiler_params=pltpu.CompilerParams(
            collective_id=0, has_side_effects=True, vmem_limit_bytes=63 * 1024 * 1024
        ),
    )(
        features.reshape(half, count),
        out_grad.reshape(half, count),
        cheb_weights,
        band_offsets.T,
        edge_weight.T,
    )
    if not fused:
        weight = lax.psum(weight, "patch") * (1.0 / pixels**0.5)
        near = weight[0]
        far = lax.ppermute(weight[1], "chan", [(0, 1), (1, 0)])
        first = lax.axis_index("chan") == 0
        weight = jnp.where(
            first, jnp.concatenate([near, far], axis=2), jnp.concatenate([far, near], axis=2)
        ).astype(BF16)
    return grad.reshape(half, 1, count), weight


def solution(mesh):
    placed = (
        P("chan", "maps", "patch"),
        P("chan", "maps", "patch"),
        P(None, "chan", None),
        P("patch", None),
        P("patch", None),
    )
    return jax.shard_map(
        on_device,
        mesh=mesh,
        in_specs=placed,
        out_specs=(P("chan", "maps", "patch"), P("maps", "chan", None)),
        check_vma=False,
    )
```
